32 devices in a mesh: seq: 8 (over y, x, core), head: 4 (over z).
Axes of the slice: x: 2, y: 2, z: 4, core: 2. Of those that a mesh axis runs over, the one named last changes fastest.
Arguments:
- queries: bfloat16 [1024, 4096], P('seq', 'head'), may hold values from -500 to 500
- first_key_rows: bfloat16 [1024, 2048], P('seq', 'head'), may hold values from -6 to 6
- first_value_rows: bfloat16 [1024, 2048], P('seq', 'head'), may hold values from -6 to 6
- second_key_rows: bfloat16 [1024, 2048], P('seq', 'head'), may hold values from -6 to 6
- second_value_rows: bfloat16 [1024, 2048], P('seq', 'head'), may hold values from -6 to 6
- out_weight: bfloat16 [4096, 4096], P('head'), may hold values from -6 to 6
Outputs:
- projected: bfloat16 [1024, 4096], P('seq', 'head')
The draws below stay inside these ranges and needn't reach their ends.
All inputs are finite; a program needn't handle non-finite values.
Results may differ from the reference program's by a relative error of at most 0.015.
The reference program's roundings to bfloat16 on the way count: a program that leaves them out, or rounds other values in their place, can miss the bound.
Values may be sent and summed in bfloat16 or wider, within the bound.
A program may use at most 64 MiB of HBM per device.

```python
import jax
import jax.numpy as jnp
from jax import lax

D = 4096
QUERY_HEADS = 32
KEY_VALUE_HEADS = 16
HEAD_SIZE = 128
W1 = 512
W2 = 32
R = 128
TOTAL_TOKENS = 1024
N_HEAD = 4


def draw_queries(key, part):
    key_base = jax.random.fold_in(key, 0)
    values_drawn = jnp.clip(jax.random.normal(key_base, (TOTAL_TOKENS, QUERY_HEADS * HEAD_SIZE), jnp.float32), -6.0, 6.0)
    return values_drawn.astype(jnp.bfloat16)


def level_of(rng, shape, cuts, least, high):
    gain, own = 1.0, jax.random.fold_in(rng, 6)
    for dim, blocks in cuts:
        heights = jnp.exp(jax.random.uniform(jax.random.fold_in(own, dim), (blocks,), jnp.float32, least / len(cuts), high / len(cuts)))
        gain = gain * jnp.repeat(heights, shape[dim] // blocks).reshape([-1 if axis == dim else 1 for axis in range(len(shape))])
    return gain


def gaussian(rng, shape, deviation, most, pieces=(), held_as=jnp.bfloat16):
    result = deviation * jax.random.normal(rng, shape, jnp.float32)
    if pieces:
        result = result * level_of(rng, shape, pieces, -0.22, 0.18)
    return jnp.clip(result, -most, most).astype(held_as)


def setup_inputs(seed: int = 0) -> dict:
    key_of = jax.random.split(jax.random.key(seed), 7)
    return {
        "queries": draw_queries(jax.random.fold_in(key_of[6], 71), 0),
        "first_key_rows": gaussian(key_of[1], (TOTAL_TOKENS, KEY_VALUE_HEADS * HEAD_SIZE), 1.0, 6.0, ((0, 8), (1, 4))),
        "first_value_rows": gaussian(key_of[2], (TOTAL_TOKENS, KEY_VALUE_HEADS * HEAD_SIZE), 1.0, 6.0, ((0, 8), (1, 4))),
        "second_key_rows": gaussian(key_of[3], (TOTAL_TOKENS, KEY_VALUE_HEADS * HEAD_SIZE), 1.0, 6.0, ((0, 8), (1, 4))),
        "second_value_rows": gaussian(key_of[4], (TOTAL_TOKENS, KEY_VALUE_HEADS * HEAD_SIZE), 1.0, 6.0, ((0, 8), (1, 4))),
        "out_weight": gaussian(key_of[5], (QUERY_HEADS * HEAD_SIZE, D), 1.0, 6.0, ((0, 4),)),
    }


def window_attend(query_block, outer_keys, outer_values, inner_keys, inner_values, first_pos):
    row_count = query_block.shape[0]
    inner_span = inner_keys.shape[0] - row_count
    outer_span = outer_keys.shape[0] - row_count
    scale_factor = query_block.shape[1] ** -0.5
    inner_key_win = jnp.stack([inner_keys[inner_span - offset:inner_span - offset + row_count] for offset in range(inner_span)])
    inner_val_win = jnp.stack([inner_values[inner_span - offset:inner_span - offset + row_count] for offset in range(inner_span)])
    blended = (query_block.astype(jnp.float32)[None] * inner_key_win.astype(jnp.float32)).astype(jnp.bfloat16)
    scores = jnp.einsum("wid,jd->wij", blended.astype(jnp.float32), outer_keys.astype(jnp.float32)) * scale_factor
    row_index = lax.broadcasted_iota(jnp.int32, scores.shape, 1)
    col_index = lax.broadcasted_iota(jnp.int32, scores.shape, 2)
    lag_index = lax.broadcasted_iota(jnp.int32, scores.shape, 0)
    allowed = (col_index > row_index) & (col_index <= row_index + outer_span)
    allowed = allowed & (first_pos - outer_span + col_index >= 0) & (first_pos + row_index - lag_index >= 0)
    scores = jnp.where(allowed, scores, -1e30)
    row_max = jnp.max(scores, axis=(0, 2), keepdims=True)
    expon = jnp.where(allowed, jnp.exp(scores - row_max), 0.0)
    row_total = jnp.sum(expon, axis=(0, 2), keepdims=True)
    weights = (expon / row_total).astype(jnp.bfloat16)
    inner_sum = jnp.einsum("wij,jd->wid", weights.astype(jnp.float32), outer_values.astype(jnp.float32))
    return jnp.sum(inner_val_win.astype(jnp.float32) * inner_sum, axis=0)


def reference(queries, first_key_rows, first_value_rows, second_key_rows, second_value_rows, out_weight):
    token_count = queries.shape[0]
    query_group_width = QUERY_HEADS // KEY_VALUE_HEADS
    block_count = token_count // R
    outer_keys_pad = jnp.pad(first_key_rows, ((W1, 0), (0, 0)))
    outer_vals_pad = jnp.pad(first_value_rows, ((W1, 0), (0, 0)))
    inner_keys_pad = jnp.pad(second_key_rows, ((W2, 0), (0, 0)))
    inner_vals_pad = jnp.pad(second_value_rows, ((W2, 0), (0, 0)))

    def per_head(head):
        kv_start = (head // query_group_width) * HEAD_SIZE
        query_cols = lax.dynamic_slice_in_dim(queries, head * HEAD_SIZE, HEAD_SIZE, 1)
        key_one = lax.dynamic_slice_in_dim(outer_keys_pad, kv_start, HEAD_SIZE, 1)
        val_one = lax.dynamic_slice_in_dim(outer_vals_pad, kv_start, HEAD_SIZE, 1)
        key_two = lax.dynamic_slice_in_dim(inner_keys_pad, kv_start, HEAD_SIZE, 1)
        val_two = lax.dynamic_slice_in_dim(inner_vals_pad, kv_start, HEAD_SIZE, 1)

        def per_block(block):
            first_pos = block * R
            return window_attend(
                lax.dynamic_slice_in_dim(query_cols, first_pos, R, 0),
                lax.dynamic_slice_in_dim(key_one, first_pos, W1 + R, 0),
                lax.dynamic_slice_in_dim(val_one, first_pos, W1 + R, 0),
                lax.dynamic_slice_in_dim(key_two, first_pos, W2 + R, 0),
                lax.dynamic_slice_in_dim(val_two, first_pos, W2 + R, 0),
                first_pos).astype(jnp.bfloat16)

        return lax.map(per_block, jnp.arange(block_count, dtype=jnp.int32)).reshape(token_count, HEAD_SIZE)

    heads_out = lax.map(per_head, jnp.arange(QUERY_HEADS, dtype=jnp.int32))
    attended = jnp.transpose(heads_out, (1, 0, 2)).reshape(token_count, QUERY_HEADS * HEAD_SIZE)
    group_rows = QUERY_HEADS * HEAD_SIZE // N_HEAD
    summed = jnp.zeros((token_count, D), jnp.float32)
    for group in range(N_HEAD):
        part_term = jnp.dot(attended[:, group * group_rows:(group + 1) * group_rows],
                            out_weight[group * group_rows:(group + 1) * group_rows],
                            preferred_element_type=jnp.float32)
        summed = summed + lax.optimization_barrier(part_term.astype(jnp.bfloat16)).astype(jnp.float32)
    return summed.astype(jnp.bfloat16)
```

```python
import functools
import math

import jax
import jax.numpy as jnp
from jax import lax
from jax.experimental import pallas as pl
from jax.experimental.pallas import tpu as pltpu
from jax.sharding import PartitionSpec as P

HEAD_SIZE = 128
W1 = 512
W2 = 32
LAGS_PER_STEP = 2


def from_behind(shard, axis, by):
    length = lax.axis_size(axis)
    pairs = [(i, i + by) for i in range(length) if 0 <= i + by < length]
    return lax.ppermute(shard, axis, pairs)


def attend_kernel(
    query_ref, key_ref, value_ref, inner_key_ref, inner_value_ref, out_ref,
    keys, values, inner_keys, inner_values, inner_counts, scores,
):
    rows = query_ref.shape[0]
    heads = query_ref.shape[1] // HEAD_SIZE
    prior = key_ref.shape[0] // rows - 1
    middle = (prior - 1) * rows
    width = prior * rows
    span = inner_key_ref.shape[0] - rows
    steps = span // LAGS_PER_STEP
    step_rows = LAGS_PER_STEP * rows
    factor = HEAD_SIZE ** (-0.5) * math.log2(math.e)
    shard = lax.axis_index("seq")
    missing = jnp.maximum(prior - shard, 0)

    first_key = key_ref[pl.ds(pl.multiple_of(missing * rows, rows), 16), :][:1]
    for block in range(prior + 1):
        here = slice(block * rows, (block + 1) * rows)
        present = (block >= missing) if block < prior else None
        key_block, value_block = key_ref[here, :], value_ref[here, :]
        count = jnp.ones((rows, HEAD_SIZE), jnp.bfloat16)
        if present is not None:
            key_block = jnp.where(present, key_block, jnp.broadcast_to(first_key, key_block.shape))
            value_block = jnp.where(present, value_block, jnp.zeros_like(value_block))
            count = jnp.where(present, count, jnp.zeros_like(count))
        to = {0: 0, prior: 1}.get(block, block + 1)
        there = slice(to * rows, (to + 1) * rows)
        keys[there, :] = key_block
        values[there, :HEAD_SIZE] = value_block
        values[there, HEAD_SIZE:] = count

    inner_keys[...] = inner_key_ref[...].astype(jnp.float32)
    inner_values[...] = inner_value_ref[...].astype(jnp.float32)
    inner_counts[...] = jnp.ones((span + rows, HEAD_SIZE), jnp.float32)

    @pl.when(shard == 0)
    def _():
        inner_keys[:span, :] = jnp.broadcast_to(inner_keys[span : span + 1, :], (span, HEAD_SIZE))
        inner_values[:span, :] = jnp.zeros((span, HEAD_SIZE), jnp.float32)
        inner_counts[:span, :] = jnp.zeros((span, HEAD_SIZE), jnp.float32)

    row_index = lax.broadcasted_iota(jnp.int32, (rows, rows), 0)
    col_index = lax.broadcasted_iota(jnp.int32, (rows, rows), 1)
    oldest = col_index > row_index
    contract_last = (((1,), (1,)), ((), ()))

    def score_step(step, tops):
        blended = []
        for head in range(heads):
            query = query_ref[:, head * HEAD_SIZE : (head + 1) * HEAD_SIZE].astype(jnp.float32)
            for i in range(LAGS_PER_STEP):
                lag = step * LAGS_PER_STEP + i
                window = inner_keys[pl.ds(span - lag, rows), :]
                blended.append((query * window).astype(jnp.bfloat16))
        blended = jnp.concatenate(blended, axis=0)
        edge = lax.dot_general(
            blended, keys[: 2 * rows, :], contract_last, preferred_element_type=jnp.float32
        )
        rest = lax.dot_general(
            blended, keys[2 * rows :, :], contract_last, preferred_element_type=jnp.float32
        )
        result = []
        for head in range(heads):
            top = tops[head]
            for i in range(LAGS_PER_STEP):
                at = slice((head * LAGS_PER_STEP + i) * rows, (head * LAGS_PER_STEP + i + 1) * rows)
                both = jnp.where(oldest, edge[at, :rows], edge[at, rows:])
                to = pl.ds(pl.multiple_of((step * LAGS_PER_STEP + i) * rows, rows), rows)
                scores[head, to, :rows] = both
                scores[head, to, rows:] = rest[at, :]
                top = jnp.maximum(top, both)
                for block in range(prior - 1):
                    top = jnp.maximum(top, rest[at, block * rows : (block + 1) * rows])
            result.append(top)
        return tuple(result)

    lowest = jnp.full((rows, rows), -jnp.inf, jnp.float32)
    tops = lax.fori_loop(0, steps, score_step, (lowest,) * heads)
    tops = [
        jnp.broadcast_to(jnp.max(top, axis=1, keepdims=True), (rows, HEAD_SIZE)) for top in tops
    ]

    def value_step(step, totals):
        weights = []
        for head in range(heads):
            for i in range(LAGS_PER_STEP):
                at = pl.ds(pl.multiple_of((step * LAGS_PER_STEP + i) * rows, rows), rows)
                parts = []
                for block in range(prior):
                    part = scores[head, at, block * rows : (block + 1) * rows]
                    parts.append(jnp.exp2((part - tops[head]) * factor))
                edge = parts[0]
                parts = [jnp.where(oldest, edge, 0.0), jnp.where(oldest, 0.0, edge)] + parts[1:]
                weights.append(jnp.concatenate([part.astype(jnp.bfloat16) for part in parts], axis=1))
        weights = jnp.concatenate(weights, axis=0)
        summed = jnp.dot(weights, values[...], preferred_element_type=jnp.float32)
        result = []
        for head in range(heads):
            total, count = totals[head]
            for i in range(LAGS_PER_STEP):
                window = pl.ds(span - step * LAGS_PER_STEP - i, rows)
                at = slice((head * LAGS_PER_STEP + i) * rows, (head * LAGS_PER_STEP + i + 1) * rows)
                total = total + inner_values[window, :] * summed[at, :HEAD_SIZE]
                count = count + inner_counts[window, :] * summed[at, HEAD_SIZE:]
            result.append((total, count))
        return tuple(result)

    nothing = jnp.zeros((rows, HEAD_SIZE), jnp.float32)
    totals = lax.fori_loop(0, steps, value_step, ((nothing, nothing),) * heads)
    for head in range(heads):
        total, count = totals[head]
        out_ref[:, head * HEAD_SIZE : (head + 1) * HEAD_SIZE] = (total / count).astype(out_ref.dtype)


def attend(queries, keys, values, inner_keys, inner_values):
    rows = queries.shape[0]
    groups = keys.shape[1] // HEAD_SIZE
    heads = queries.shape[1] // keys.shape[1]
    outer = keys.shape[0]
    inner = inner_keys.shape[0]
    span = inner - rows
    width = outer - rows
    column = lambda g: (0, g)
    pairs = heads * groups * span * rows
    return pl.pallas_call(
        attend_kernel,
        grid=(groups,),
        out_shape=jax.ShapeDtypeStruct(queries.shape, queries.dtype),
        in_specs=[
            pl.BlockSpec((rows, heads * HEAD_SIZE), column),
            pl.BlockSpec((outer, HEAD_SIZE), column),
            pl.BlockSpec((outer, HEAD_SIZE), column),
            pl.BlockSpec((inner, HEAD_SIZE), column),
            pl.BlockSpec((inner, HEAD_SIZE), column),
        ],
        out_specs=pl.BlockSpec((rows, heads * HEAD_SIZE), column),
        scratch_shapes=[
            pltpu.VMEM((outer, HEAD_SIZE), jnp.bfloat16),
            pltpu.VMEM((outer, 2 * HEAD_SIZE), jnp.bfloat16),
            pltpu.VMEM((inner, HEAD_SIZE), jnp.float32),
            pltpu.VMEM((inner, HEAD_SIZE), jnp.float32),
            pltpu.VMEM((inner, HEAD_SIZE), jnp.float32),
            pltpu.VMEM((heads, span * rows, width), jnp.float32),
        ],
        compiler_params=pltpu.CompilerParams(vmem_limit_bytes=48 * 1024 * 1024),
        cost_estimate=pl.CostEstimate(
            flops=4 * pairs * outer * HEAD_SIZE,
            bytes_accessed=4 * queries.size + 4 * keys.size,
            transcendentals=pairs * width,
        ),
    )(queries, keys, values, inner_keys, inner_values)


def local(
    queries, first_key_rows, first_value_rows, second_key_rows, second_value_rows, out_weight
):
    row_count = queries.shape[0]
    shard_count = W1 // row_count
    prior_inner = from_behind(
        (second_key_rows[row_count - W2 :], second_value_rows[row_count - W2 :]), "seq", 1
    )
    pieces_keys = []
    pieces_values = []
    for distance in range(shard_count, 0, -1):
        arrived = from_behind((first_key_rows, first_value_rows), "seq", distance)
        pieces_keys.append(arrived[0])
        pieces_values.append(arrived[1])
    keys = jnp.concatenate(pieces_keys + [first_key_rows], axis=0)
    values = jnp.concatenate(pieces_values + [first_value_rows], axis=0)
    inner_keys = jnp.concatenate([prior_inner[0], second_key_rows], axis=0)
    inner_values = jnp.concatenate([prior_inner[1], second_value_rows], axis=0)
    attended = attend(queries, keys, values, inner_keys, inner_values)
    partial = jnp.dot(attended, out_weight, preferred_element_type=jnp.float32).astype(jnp.bfloat16)
    return lax.psum_scatter(partial, "head", scatter_dimension=1, tiled=True)


def solution(mesh):
    in_specs = (P("seq", "head"),) * 5 + (P("head", None),)
    return jax.shard_map(
        local, mesh=mesh, in_specs=in_specs, out_specs=P("seq", "head"), check_vma=False
    )
```

```python
import functools
import math

import jax
import jax.numpy as jnp
from jax import lax
from jax.experimental import pallas as pl
from jax.experimental.pallas import tpu as pltpu
from jax.sharding import PartitionSpec as P

HEAD_SIZE = 128
W1 = 512
W2 = 32
CHUNK_ROWS = 64
LAGS_PER_STEP = 4
MESH = pl.DeviceIdType.MESH


def layer_kernel(
    shards, owners,
    query_ref, key_ref, value_ref, inner_key_ref, inner_value_ref, weight_hbm, out_ref,
    outer, tail_keys, tail_values, inner_keys, inner_values, inner_counts,
    scores, attended, weight, partial, landed,
    outer_send, outer_recv, tail_send, tail_recv, part_send, part_recv, weight_sem,
):
    rows = query_ref.shape[0]
    groups = key_ref.shape[1] // HEAD_SIZE
    heads = query_ref.shape[1] // key_ref.shape[1]
    prior = outer.shape[1] // rows - 1
    span = tail_keys.shape[0]
    chunks = rows // CHUNK_ROWS
    steps = span // LAGS_PER_STEP
    own_width = out_ref.shape[1]
    factor = HEAD_SIZE ** (-0.5) * math.log2(math.e)
    shard = lax.axis_index("seq")
    owner = lax.axis_index("head")

    weight_copy = pltpu.make_async_copy(weight_hbm, weight, weight_sem)
    weight_copy.start()

    barrier = pltpu.get_barrier_semaphore()
    for distance in range(1, prior + 1):
        for to in (shard + distance, shard + shards - distance):
            pl.semaphore_signal(
                barrier, inc=1, device_id={"seq": lax.rem(to, shards)}, device_id_type=MESH
            )
    for offset in range(1, owners):
        pl.semaphore_signal(
            barrier, inc=1, device_id={"head": lax.rem(owner + offset, owners)}, device_id_type=MESH
        )

    def slot_of(block):
        return {0: 0, prior: 1}.get(block, block + 1)

    def block_rows(block):
        return pl.ds(slot_of(block) * rows, rows)

    own = block_rows(prior)
    for group in range(groups):
        columns = slice(group * HEAD_SIZE, (group + 1) * HEAD_SIZE)
        outer[group, own, :HEAD_SIZE] = key_ref[:, columns]
        outer[group, own, HEAD_SIZE : 2 * HEAD_SIZE] = value_ref[:, columns]
        outer[group, :, 2 * HEAD_SIZE :] = jnp.ones((outer.shape[1], HEAD_SIZE), jnp.bfloat16)

    pl.semaphore_wait(barrier, 2 * prior + owners - 1)

    def tail_copy(which):
        source, target = ((inner_key_ref, tail_keys), (inner_value_ref, tail_values))[which]
        return pltpu.make_async_remote_copy(
            src_ref=source.at[pl.ds(rows - span, span), :],
            dst_ref=target,
            send_sem=tail_send.at[which],
            recv_sem=tail_recv.at[which],
            device_id={"seq": lax.rem(shard + 1, shards)},
            device_id_type=MESH,
        )

    def outer_copy(group, distance):
        keys_values = pl.ds(0, 2 * HEAD_SIZE)
        return pltpu.make_async_remote_copy(
            src_ref=outer.at[group, own, keys_values],
            dst_ref=outer.at[group, block_rows(prior - distance), keys_values],
            send_sem=outer_send.at[group, distance - 1],
            recv_sem=outer_recv.at[group, distance - 1],
            device_id={"seq": lax.rem(shard + distance, shards)},
            device_id_type=MESH,
        )

    @pl.when(shard + 1 < shards)
    def _():
        tail_copy(0).start()
        tail_copy(1).start()

    for group in range(groups):
        for distance in range(prior, 0, -1):
            @pl.when(shard + distance < shards)
            def _():
                outer_copy(group, distance).start()

    for group in range(groups):
        columns = slice(group * HEAD_SIZE, (group + 1) * HEAD_SIZE)
        inner_keys[group, span:, :] = inner_key_ref[:, columns].astype(jnp.float32)
        inner_values[group, span:, :] = inner_value_ref[:, columns].astype(jnp.float32)
    inner_counts[...] = jnp.ones(inner_counts.shape, jnp.float32)

    @pl.when(shard == 0)
    def _():
        for group in range(groups):
            first = inner_keys[group, span : span + 1, :]
            inner_keys[group, :span, :] = jnp.broadcast_to(first, (span, HEAD_SIZE))
            inner_values[group, :span, :] = jnp.zeros((span, HEAD_SIZE), jnp.float32)
        inner_counts[:span, :] = jnp.zeros((span, HEAD_SIZE), jnp.float32)

    @pl.when(shard > 0)
    def _():
        tail_copy(0).wait_recv()
        tail_copy(1).wait_recv()
        for group in range(groups):
            columns = slice(group * HEAD_SIZE, (group + 1) * HEAD_SIZE)
            inner_keys[group, :span, :] = tail_keys[:, columns].astype(jnp.float32)
            inner_values[group, :span, :] = tail_values[:, columns].astype(jnp.float32)

    def receive(group):
        for distance in range(1, prior + 1):
            @pl.when(shard >= distance)
            def _():
                outer_copy(group, distance).wait_recv()

        for place in range(prior):
            @pl.when(shard == place)
            def _():
                first = outer[group, block_rows(prior - place), :HEAD_SIZE][:1]
                for block in range(prior - place):
                    outer[group, block_rows(block), :HEAD_SIZE] = jnp.broadcast_to(
                        first, (rows, HEAD_SIZE)
                    )
                    outer[group, block_rows(block), HEAD_SIZE:] = jnp.zeros(
                        (rows, 2 * HEAD_SIZE), jnp.bfloat16
                    )

    row_index = lax.broadcasted_iota(jnp.int32, (CHUNK_ROWS, rows), 0)
    col_index = lax.broadcasted_iota(jnp.int32, (CHUNK_ROWS, rows), 1)
    ahead = col_index - row_index
    contract_last = (((1,), (1,)), ((), ()))

    def place_of(item):
        group = lax.rem(item, groups)
        first_row = pl.multiple_of(lax.div(item, groups) * CHUNK_ROWS, CHUNK_ROWS)
        return group, first_row

    def part_rows(head, i):
        start = (head * LAGS_PER_STEP + i) * CHUNK_ROWS
        return slice(start, start + CHUNK_ROWS)

    def score_rows(step, i):
        return pl.ds(pl.multiple_of((step * LAGS_PER_STEP + i) * CHUNK_ROWS, CHUNK_ROWS), CHUNK_ROWS)

    def score_step(item, step, tops):
        group, first_row = place_of(item)
        oldest = ahead > first_row
        blended = []
        for head in range(heads):
            columns = pl.ds(
                pl.multiple_of((group * heads + head) * HEAD_SIZE, HEAD_SIZE), HEAD_SIZE
            )
            query = query_ref[pl.ds(first_row, CHUNK_ROWS), columns].astype(jnp.float32)
            for i in range(LAGS_PER_STEP):
                start = span + first_row - step * LAGS_PER_STEP - i
                window = inner_keys[group, pl.ds(start, CHUNK_ROWS), :]
                blended.append((query * window).astype(jnp.bfloat16))
        blended = jnp.concatenate(blended, axis=0)
        keys = outer[group, :, :HEAD_SIZE]
        edge = lax.dot_general(
            blended, keys[: 2 * rows], contract_last, preferred_element_type=jnp.float32
        )
        rest = lax.dot_general(
            blended, keys[2 * rows :], contract_last, preferred_element_type=jnp.float32
        )
        result = []
        for head in range(heads):
            top = tops[head]
            for i in range(LAGS_PER_STEP):
                at = part_rows(head, i)
                both = jnp.where(oldest, edge[at, :rows], edge[at, rows:])
                scores[head, score_rows(step, i), :rows] = both
                scores[head, score_rows(step, i), rows:] = rest[at, :]
                top = jnp.maximum(top, both)
                for block in range(prior - 1):
                    top = jnp.maximum(top, rest[at, block * rows : (block + 1) * rows])
            result.append(top)
        return tuple(result)

    def load_weights(item, step, tops):
        _, first_row = place_of(item)
        oldest = ahead > first_row
        weights = []
        for head in range(heads):
            for i in range(LAGS_PER_STEP):
                parts = []
                for block in range(prior):
                    part = scores[head, score_rows(step, i), block * rows : (block + 1) * rows]
                    parts.append(jnp.exp2((part - tops[head]) * factor))
                edge = parts[0]
                parts = [jnp.where(oldest, edge, 0.0), jnp.where(oldest, 0.0, edge)] + parts[1:]
                weights.append(jnp.concatenate([part.astype(jnp.bfloat16) for part in parts], axis=1))
        return jnp.concatenate(weights, axis=0)

    def value_step(item, step, tops, totals):
        group, first_row = place_of(item)
        weights = load_weights(item, step, tops)
        summed = jnp.dot(
            weights, outer[group, :, HEAD_SIZE:], preferred_element_type=jnp.float32
        )
        result = []
        for head in range(heads):
            total, count = totals[head]
            for i in range(LAGS_PER_STEP):
                window = pl.ds(span + first_row - step * LAGS_PER_STEP - i, CHUNK_ROWS)
                at = part_rows(head, i)
                total = total + inner_values[group, window, :] * summed[at, :HEAD_SIZE]
                count = count + inner_counts[window, :] * summed[at, HEAD_SIZE:]
            result.append((total, count))
        return tuple(result)

    lowest = (jnp.full((CHUNK_ROWS, rows), -jnp.inf, jnp.float32),) * heads
    zero = jnp.zeros((CHUNK_ROWS, HEAD_SIZE), jnp.float32)
    nothing = ((zero, zero),) * heads

    def finish_tops(tops):
        return tuple(
            jnp.broadcast_to(jnp.max(top, axis=1, keepdims=True), (CHUNK_ROWS, HEAD_SIZE))
            for top in tops
        )

    def part_copy(offset, first_row):
        chunk = lax.div(first_row, CHUNK_ROWS)
        at = pl.ds(first_row, CHUNK_ROWS)
        return pltpu.make_async_remote_copy(
            src_ref=partial.at[offset, at, :],
            dst_ref=landed.at[offset - 1, at, :],
            send_sem=part_send.at[offset - 1, chunk],
            recv_sem=part_recv.at[offset - 1, chunk],
            device_id={"head": lax.rem(owner + offset, owners)},
            device_id_type=MESH,
        )

    def finish_item(item, totals):
        group, first_row = place_of(item)
        for head in range(heads):
            total, count = totals[head]
            columns = pl.ds(
                pl.multiple_of((group * heads + head) * HEAD_SIZE, HEAD_SIZE), HEAD_SIZE
            )
            attended[:, columns] = (total / count).astype(jnp.bfloat16)

        @pl.when(group == groups - 1)
        def _():
            @pl.when(first_row == 0)
            def _():
                weight_copy.wait()

            for offset in list(range(1, owners)) + [0]:
                to = lax.rem(owner + offset, owners)
                columns = pl.ds(pl.multiple_of(to * own_width, own_width), own_width)
                partial[offset, pl.ds(first_row, CHUNK_ROWS), :] = jnp.dot(
                    attended[...], weight[:, columns], preferred_element_type=jnp.float32
                ).astype(jnp.bfloat16)
                if offset:
                    part_copy(offset, first_row).start()

    receive(0)
    tops = lax.fori_loop(0, steps, lambda step, tops: score_step(0, step, tops), lowest)

    def both_passes(item, tops):
        for group in range(1, groups):
            @pl.when(item == group)
            def _():
                receive(group)

        before = finish_tops(tops)

        def step_of(step, carry):
            now, totals = carry
            totals = value_step(item - 1, step, before, totals)
            return score_step(item, step, now), totals

        tops, totals = lax.fori_loop(0, steps, step_of, (lowest, nothing))
        finish_item(item - 1, totals)
        return tops

    items = groups * chunks
    tops = lax.fori_loop(1, items, both_passes, tops)
    before = finish_tops(tops)
    totals = lax.fori_loop(
        0, steps, lambda step, totals: value_step(items - 1, step, before, totals), nothing
    )
    finish_item(items - 1, totals)

    for group in range(groups):
        for distance in range(1, prior + 1):
            @pl.when(shard + distance < shards)
            def _():
                outer_copy(group, distance).wait_send()

    @pl.when(shard + 1 < shards)
    def _():
        tail_copy(0).wait_send()
        tail_copy(1).wait_send()

    for chunk in range(chunks):
        first_row = chunk * CHUNK_ROWS
        at = pl.ds(first_row, CHUNK_ROWS)
        total = partial[0, at, :].astype(jnp.float32)
        for offset in range(1, owners):
            part_copy(offset, first_row).wait_recv()
            total = total + landed[offset - 1, at, :].astype(jnp.float32)
        out_ref[at, :] = total.astype(out_ref.dtype)
    for chunk in range(chunks):
        for offset in range(1, owners):
            part_copy(offset, chunk * CHUNK_ROWS).wait_send()


def local(shards, owners, queries, first_keys, first_values, inner_keys, inner_values, out_weight):
    rows = queries.shape[0]
    groups = first_keys.shape[1] // HEAD_SIZE
    heads = queries.shape[1] // first_keys.shape[1]
    prior = W1 // rows
    outer = W1 + rows
    inner = W2 + rows
    features = out_weight.shape[1]
    chunks = rows // CHUNK_ROWS
    pairs = heads * groups * W2 * rows
    vmem = pl.BlockSpec(memory_space=pltpu.VMEM)
    dma = pltpu.SemaphoreType.DMA
    return pl.pallas_call(
        functools.partial(layer_kernel, shards, owners),
        out_shape=jax.ShapeDtypeStruct((rows, features // owners), queries.dtype),
        in_specs=[vmem] * 5 + [pl.BlockSpec(memory_space=pl.ANY)],
        out_specs=vmem,
        scratch_shapes=[
            pltpu.VMEM((groups, outer, 3 * HEAD_SIZE), jnp.bfloat16),
            pltpu.VMEM((W2, groups * HEAD_SIZE), jnp.bfloat16),
            pltpu.VMEM((W2, groups * HEAD_SIZE), jnp.bfloat16),
            pltpu.VMEM((groups, inner, HEAD_SIZE), jnp.float32),
            pltpu.VMEM((groups, inner, HEAD_SIZE), jnp.float32),
            pltpu.VMEM((inner, HEAD_SIZE), jnp.float32),
            pltpu.VMEM((heads, W2 * CHUNK_ROWS, W1), jnp.float32),
            pltpu.VMEM((CHUNK_ROWS, queries.shape[1]), jnp.bfloat16),
            pltpu.VMEM(out_weight.shape, jnp.bfloat16),
            pltpu.VMEM((owners, rows, features // owners), jnp.bfloat16),
            pltpu.VMEM((owners - 1, rows, features // owners), jnp.bfloat16),
            dma((groups, prior)),
            dma((groups, prior)),
            dma((2,)),
            dma((2,)),
            dma((owners - 1, chunks)),
            dma((owners - 1, chunks)),
            dma(()),
        ],
        compiler_params=pltpu.CompilerParams(
            collective_id=0, has_side_effects=True, vmem_limit_bytes=48 * 1024 * 1024
        ),
        cost_estimate=pl.CostEstimate(
            flops=4 * pairs * outer * HEAD_SIZE + 2 * rows * out_weight.size,
            bytes_accessed=2 * out_weight.size,
            transcendentals=pairs * W1,
        ),
    )(queries, first_keys, first_values, inner_keys, inner_values, out_weight)


def solution(mesh):
    in_specs = (P("seq", "head"),) * 5 + (P("head", None),)
    return jax.shard_map(
        functools.partial(local, mesh.shape["seq"], mesh.shape["head"]),
        mesh=mesh, in_specs=in_specs, out_specs=P("seq", "head"), check_vma=False,
    )
```

```python
import functools
import math

import jax
import jax.numpy as jnp
from jax import lax
from jax.experimental import pallas as pl
from jax.experimental.pallas import tpu as pltpu
from jax.sharding import PartitionSpec as P

HEAD_SIZE = 128
W1 = 512
W2 = 32
CHUNK_ROWS = 64
LAGS_PER_STEP = 4
MESH = pl.DeviceIdType.MESH


def layer_kernel(
    shards, owners,
    query_hbm, key_hbm, value_hbm, inner_key_hbm, inner_value_hbm, weight_hbm, out_ref,
    query_ref, inner_key_ref, inner_value_ref,
    outer, flipped, tail_keys, tail_values, inner_keys, inner_values,
    scores, attended, weight, partial, landed,
    outer_send, outer_recv, tail_send, tail_recv, part_send, part_recv, weight_sem, load_sem, own_sem,
):
    rows = query_ref.shape[0]
    groups = outer.shape[0]
    heads = query_ref.shape[1] // (groups * HEAD_SIZE)
    prior = outer.shape[1] // rows - 1
    span = tail_keys.shape[0]
    chunks = rows // CHUNK_ROWS
    steps = span // LAGS_PER_STEP
    own_width = out_ref.shape[1]
    factor = HEAD_SIZE ** (-0.5) * math.log2(math.e)
    shard = lax.axis_index("seq")
    owner = lax.axis_index("head")

    barrier = pltpu.get_barrier_semaphore()
    for distance in range(1, prior + 1):
        for to in (shard + distance, shard + shards - distance):
            pl.semaphore_signal(
                barrier, inc=1, device_id={"seq": lax.rem(to, shards)}, device_id_type=MESH
            )
    for offset in range(1, owners):
        pl.semaphore_signal(
            barrier, inc=1, device_id={"head": lax.rem(owner + offset, owners)}, device_id_type=MESH
        )

    def slot_of(block):
        return {0: 0, prior: 1}.get(block, block + 1)

    def block_rows(block):
        return pl.ds(slot_of(block) * rows, rows)

    own = block_rows(prior)

    def own_copy(group, which):
        return pltpu.make_async_copy(
            (key_hbm, value_hbm)[which].at[:, pl.ds(group * HEAD_SIZE, HEAD_SIZE)],
            outer.at[group, own, pl.ds(which * HEAD_SIZE, HEAD_SIZE)],
            own_sem.at[group, which],
        )

    loads = [
        pltpu.make_async_copy(source, target, load_sem.at[i])
        for i, (source, target) in enumerate((
            (inner_key_hbm, inner_key_ref), (inner_value_hbm, inner_value_ref),
            (query_hbm, query_ref),
        ))
    ]
    for load in loads:
        load.start()
    for group in range(groups):
        for which in range(2):
            own_copy(group, which).start()
    weight_copy = pltpu.make_async_copy(weight_hbm, weight, weight_sem)
    weight_copy.start()
    for load in loads:
        load.wait()
    for group in range(groups):
        for which in range(2):
            own_copy(group, which).wait()

    pl.semaphore_wait(barrier, 2 * prior + owners - 1)

    def tail_copy(which):
        source, target = ((inner_key_ref, tail_keys), (inner_value_ref, tail_values))[which]
        return pltpu.make_async_remote_copy(
            src_ref=source.at[pl.ds(rows - span, span), :],
            dst_ref=target,
            send_sem=tail_send.at[which],
            recv_sem=tail_recv.at[which],
            device_id={"seq": lax.rem(shard + 1, shards)},
            device_id_type=MESH,
        )

    def outer_copy(group, distance):
        keys_values = pl.ds(0, 2 * HEAD_SIZE)
        return pltpu.make_async_remote_copy(
            src_ref=outer.at[group, own, keys_values],
            dst_ref=outer.at[group, block_rows(prior - distance), keys_values],
            send_sem=outer_send.at[group, distance - 1],
            recv_sem=outer_recv.at[group, distance - 1],
            device_id={"seq": lax.rem(shard + distance, shards)},
            device_id_type=MESH,
        )

    @pl.when(shard + 1 < shards)
    def _():
        tail_copy(0).start()
        tail_copy(1).start()

    for group in range(groups):
        for distance in range(prior, 0, -1):
            @pl.when(shard + distance < shards)
            def _():
                outer_copy(group, distance).start()

    for group in range(groups):
        columns = slice(group * HEAD_SIZE, (group + 1) * HEAD_SIZE)
        inner_keys[group, span:, :] = inner_key_ref[:, columns].astype(jnp.float32)
        inner_values[group, span:, :] = inner_value_ref[:, columns].astype(jnp.float32)

    @pl.when(shard == 0)
    def _():
        for group in range(groups):
            first = inner_keys[group, span : span + 1, :]
            inner_keys[group, :span, :] = jnp.broadcast_to(first, (span, HEAD_SIZE))
            inner_values[group, :span, :] = jnp.zeros((span, HEAD_SIZE), jnp.float32)

    @pl.when(shard > 0)
    def _():
        tail_copy(0).wait_recv()
        tail_copy(1).wait_recv()
        for group in range(groups):
            columns = slice(group * HEAD_SIZE, (group + 1) * HEAD_SIZE)
            inner_keys[group, :span, :] = tail_keys[:, columns].astype(jnp.float32)
            inner_values[group, :span, :] = tail_values[:, columns].astype(jnp.float32)

    count_rows = flipped.shape[1] - HEAD_SIZE

    def flip(group, block):
        there = slice(slot_of(block) * rows, (slot_of(block) + 1) * rows)
        value = outer[group, block_rows(block), HEAD_SIZE:].astype(jnp.float32)
        flipped[group, :HEAD_SIZE, there] = value.T.astype(jnp.bfloat16)
        flipped[group, HEAD_SIZE:, there] = jnp.ones((count_rows, rows), jnp.bfloat16)

    def receive(group):
        flip(group, prior)
        for distance in range(1, prior + 1):
            @pl.when(shard >= distance)
            def _():
                outer_copy(group, distance).wait_recv()
                flip(group, prior - distance)

        for place in range(prior):
            @pl.when(shard == place)
            def _():
                first = outer[group, block_rows(prior - place), :HEAD_SIZE][:1]
                for block in range(prior - place):
                    there = slice(slot_of(block) * rows, (slot_of(block) + 1) * rows)
                    outer[group, block_rows(block), :HEAD_SIZE] = jnp.broadcast_to(
                        first, (rows, HEAD_SIZE)
                    )
                    flipped[group, :, there] = jnp.zeros((flipped.shape[1], rows), jnp.bfloat16)

    lanes = LAGS_PER_STEP * CHUNK_ROWS
    pair_index = lax.broadcasted_iota(jnp.int32, (rows, lanes), 1)
    ahead = lax.broadcasted_iota(jnp.int32, (rows, lanes), 0) - lax.rem(pair_index, CHUNK_ROWS)
    pair_index = lax.broadcasted_iota(jnp.int32, (8, lanes), 1)
    behind = lax.rem(pair_index, CHUNK_ROWS) - lax.div(pair_index, CHUNK_ROWS)
    contract_last = (((1,), (1,)), ((), ()))

    def place_of(item):
        group = lax.rem(item, groups)
        first_row = pl.multiple_of(lax.div(item, groups) * CHUNK_ROWS, CHUNK_ROWS)
        return group, first_row

    def windows_of(array, group, first_row, step):
        start = span + first_row - step * LAGS_PER_STEP
        return [array[group, pl.ds(start - i, CHUNK_ROWS), :] for i in range(LAGS_PER_STEP)]

    def head_columns(group, head):
        return pl.ds(pl.multiple_of((group * heads + head) * HEAD_SIZE, HEAD_SIZE), HEAD_SIZE)

    def by_eight(array):
        return array.reshape(array.shape[0] // 8, 8, array.shape[1])

    def score_step(item, step, tops):
        group, first_row = place_of(item)
        oldest = ahead > first_row
        windows = windows_of(inner_keys, group, first_row, step)
        keys = outer[group, :, :HEAD_SIZE]
        result = []
        for head in range(heads):
            query = query_ref[pl.ds(first_row, CHUNK_ROWS), head_columns(group, head)]
            query = query.astype(jnp.float32)
            blended = jnp.concatenate(
                [(query * window).astype(jnp.bfloat16) for window in windows], axis=0
            )
            product = lax.dot_general(
                keys, blended, contract_last, preferred_element_type=jnp.float32
            )
            both = jnp.where(oldest, product[:rows], product[rows : 2 * rows])
            rest = product[2 * rows :]
            scores[head, step, :rows, :] = both
            scores[head, step, rows:, :] = rest
            top = jnp.maximum(jnp.max(by_eight(both), axis=0), jnp.max(by_eight(rest), axis=0))
            result.append(jnp.maximum(tops[head], top))
        return tuple(result)

    def value_step(item, step, tops, totals):
        group, first_row = place_of(item)
        oldest = ahead > first_row
        windows = jnp.concatenate(windows_of(inner_values, group, first_row, step), axis=0).T
        counted = (behind + first_row >= step * LAGS_PER_STEP) | (shard > 0)
        counted = jnp.where(counted, 1.0, 0.0)
        result = []
        for head in range(heads):
            total, count = totals[head]
            part = by_eight(scores[head, step])
            part = jnp.exp2((part - tops[head][None]) * factor).reshape(prior * rows, lanes)
            edge = part[:rows]
            weights = jnp.concatenate(
                [
                    jnp.where(oldest, edge, 0.0).astype(jnp.bfloat16),
                    jnp.where(oldest, 0.0, edge).astype(jnp.bfloat16),
                    part[rows:].astype(jnp.bfloat16),
                ],
                axis=0,
            )
            summed = jnp.dot(flipped[group], weights, preferred_element_type=jnp.float32)
            gain = windows * summed[:HEAD_SIZE]
            pairs = counted * summed[HEAD_SIZE : HEAD_SIZE + 8]
            for start in range(0, lanes, HEAD_SIZE):
                total = total + gain[:, start : start + HEAD_SIZE]
                count = count + pairs[:, start : start + HEAD_SIZE]
            result.append((total, count))
        return tuple(result)

    lowest = (jnp.full((8, lanes), -jnp.inf, jnp.float32),) * heads
    nothing = (
        (
            jnp.zeros((HEAD_SIZE, HEAD_SIZE), jnp.float32),
            jnp.zeros((8, HEAD_SIZE), jnp.float32),
        ),
    ) * heads

    def fold(array, combine):
        shift = CHUNK_ROWS
        while shift < HEAD_SIZE:
            array = combine(array, pltpu.roll(array, shift, 1))
            shift *= 2
        return array

    def finish_tops(tops):
        result = []
        for top in tops:
            most = top[:, :HEAD_SIZE]
            for start in range(HEAD_SIZE, lanes, HEAD_SIZE):
                most = jnp.maximum(most, top[:, start : start + HEAD_SIZE])
            most = jnp.max(fold(most, jnp.maximum), axis=0, keepdims=True)
            most = jnp.broadcast_to(most, (8, HEAD_SIZE))
            result.append(jnp.concatenate([most] * (lanes // HEAD_SIZE), axis=1))
        return tuple(result)

    def part_copy(offset, first_row):
        chunk = lax.div(first_row, CHUNK_ROWS)
        at = pl.ds(first_row, CHUNK_ROWS)
        return pltpu.make_async_remote_copy(
            src_ref=partial.at[offset, at, :],
            dst_ref=landed.at[offset - 1, at, :],
            send_sem=part_send.at[offset - 1, chunk],
            recv_sem=part_recv.at[offset - 1, chunk],
            device_id={"head": lax.rem(owner + offset, owners)},
            device_id_type=MESH,
        )

    def finish_item(item, totals):
        group, first_row = place_of(item)
        for head in range(heads):
            total, count = (fold(array, jnp.add) for array in totals[head])
            mean = (by_eight(total) / count[None]).reshape(total.shape).T
            attended[:, head_columns(group, head)] = mean[:CHUNK_ROWS].astype(jnp.bfloat16)

        @pl.when(group == groups - 1)
        def _():
            @pl.when(first_row == 0)
            def _():
                weight_copy.wait()

            for offset in list(range(1, owners)) + [0]:
                to = lax.rem(owner + offset, owners)
                columns = pl.ds(pl.multiple_of(to * own_width, own_width), own_width)
                partial[offset, pl.ds(first_row, CHUNK_ROWS), :] = jnp.dot(
                    attended[...], weight[:, columns], preferred_element_type=jnp.float32
                ).astype(jnp.bfloat16)
                if offset:
                    part_copy(offset, first_row).start()

    receive(0)
    tops = lax.fori_loop(0, steps, lambda step, tops: score_step(0, step, tops), lowest)

    def both_passes(item, tops):
        for group in range(1, groups):
            @pl.when(item == group)
            def _():
                receive(group)

        before = finish_tops(tops)

        def step_of(step, carry):
            now, totals = carry
            totals = value_step(item - 1, step, before, totals)
            return score_step(item, step, now), totals

        tops, totals = lax.fori_loop(0, steps, step_of, (lowest, nothing))
        finish_item(item - 1, totals)
        return tops

    items = groups * chunks
    tops = lax.fori_loop(1, items, both_passes, tops)
    before = finish_tops(tops)
    totals = lax.fori_loop(
        0, steps, lambda step, totals: value_step(items - 1, step, before, totals), nothing
    )
    finish_item(items - 1, totals)

    for group in range(groups):
        for distance in range(1, prior + 1):
            @pl.when(shard + distance < shards)
            def _():
                outer_copy(group, distance).wait_send()

    @pl.when(shard + 1 < shards)
    def _():
        tail_copy(0).wait_send()
        tail_copy(1).wait_send()

    for chunk in range(chunks):
        first_row = chunk * CHUNK_ROWS
        at = pl.ds(first_row, CHUNK_ROWS)
        total = partial[0, at, :].astype(jnp.float32)
        for offset in range(1, owners):
            part_copy(offset, first_row).wait_recv()
            total = total + landed[offset - 1, at, :].astype(jnp.float32)
        out_ref[at, :] = total.astype(out_ref.dtype)
    for chunk in range(chunks):
        for offset in range(1, owners):
            part_copy(offset, chunk * CHUNK_ROWS).wait_send()


def local(shards, owners, queries, first_keys, first_values, inner_keys, inner_values, out_weight):
    rows = queries.shape[0]
    groups = first_keys.shape[1] // HEAD_SIZE
    heads = queries.shape[1] // first_keys.shape[1]
    prior = W1 // rows
    outer = W1 + rows
    inner = W2 + rows
    features = out_weight.shape[1]
    chunks = rows // CHUNK_ROWS
    pairs = heads * groups * W2 * rows
    vmem = pl.BlockSpec(memory_space=pltpu.VMEM)
    dma = pltpu.SemaphoreType.DMA
    return pl.pallas_call(
        functools.partial(layer_kernel, shards, owners),
        out_shape=jax.ShapeDtypeStruct((rows, features // owners), queries.dtype),
        in_specs=[pl.BlockSpec(memory_space=pltpu.HBM)] * 6,
        out_specs=vmem,
        scratch_shapes=[
            pltpu.VMEM(queries.shape, jnp.bfloat16),
            pltpu.VMEM(inner_keys.shape, jnp.bfloat16),
            pltpu.VMEM(inner_keys.shape, jnp.bfloat16),
            pltpu.VMEM((groups, outer, 2 * HEAD_SIZE), jnp.bfloat16),
            pltpu.VMEM((groups, HEAD_SIZE + 16, outer), jnp.bfloat16),
            pltpu.VMEM((W2, groups * HEAD_SIZE), jnp.bfloat16),
            pltpu.VMEM((W2, groups * HEAD_SIZE), jnp.bfloat16),
            pltpu.VMEM((groups, inner, HEAD_SIZE), jnp.float32),
            pltpu.VMEM((groups, inner, HEAD_SIZE), jnp.float32),
            pltpu.VMEM(
                (heads, W2 // LAGS_PER_STEP, W1, LAGS_PER_STEP * CHUNK_ROWS), jnp.float32
            ),
            pltpu.VMEM((CHUNK_ROWS, queries.shape[1]), jnp.bfloat16),
            pltpu.VMEM(out_weight.shape, jnp.bfloat16),
            pltpu.VMEM((owners, rows, features // owners), jnp.bfloat16),
            pltpu.VMEM((owners - 1, rows, features // owners), jnp.bfloat16),
            dma((groups, prior)),
            dma((groups, prior)),
            dma((2,)),
            dma((2,)),
            dma((owners - 1, chunks)),
            dma((owners - 1, chunks)),
            dma(()),
            dma((3,)),
            dma((groups, 2)),
        ],
        compiler_params=pltpu.CompilerParams(
            collective_id=0, has_side_effects=True, vmem_limit_bytes=64 * 1024 * 1024 - 2**17
        ),
        cost_estimate=pl.CostEstimate(
            flops=4 * pairs * outer * HEAD_SIZE + 2 * rows * out_weight.size,
            bytes_accessed=2 * out_weight.size,
            transcendentals=pairs * W1,
        ),
    )(queries, first_keys, first_values, inner_keys, inner_values, out_weight)


def solution(mesh):
    in_specs = (P("seq", "head"),) * 5 + (P("head", None),)
    return jax.shard_map(
        functools.partial(local, mesh.shape["seq"], mesh.shape["head"]),
        mesh=mesh, in_specs=in_specs, out_specs=P("seq", "head"), check_vma=False,
    )
```

```python
import functools
import math

import jax
import jax.numpy as jnp
from jax import lax
from jax.experimental import pallas as pl
from jax.experimental.pallas import tpu as pltpu
from jax.sharding import PartitionSpec as P

HEAD_SIZE = 128
W1 = 512
W2 = 32
CHUNK_ROWS = 64
LAGS_PER_STEP = 4
MESH = pl.DeviceIdType.MESH


def layer_kernel(
    shards, owners,
    query_hbm, key_hbm, value_hbm, inner_key_hbm, inner_value_hbm, weight_hbm, out_ref,
    query_ref, inner_key_ref, inner_value_ref,
    outer, flipped, tail_keys, tail_values, inner_keys, inner_values,
    scores, attended, weight, partial, landed,
    outer_send, outer_recv, tail_send, tail_recv, part_send, part_recv, weight_sem, load_sem, own_sem,
    hand_send,
):
    rows = query_ref.shape[0]
    groups = outer.shape[0]
    heads = query_ref.shape[1] // (groups * HEAD_SIZE)
    prior = outer.shape[1] // rows - 1
    span = tail_keys.shape[0]
    chunks = rows // CHUNK_ROWS
    steps = span // LAGS_PER_STEP
    own_width = out_ref.shape[1]
    factor = HEAD_SIZE ** (-0.5) * math.log2(math.e)
    shard = lax.axis_index("seq")
    owner = lax.axis_index("head")

    barrier = pltpu.get_barrier_semaphore()
    direct = range(2, prior + 1, 2)
    for distance in (1, *direct):
        for to in (shard + distance, shard + shards - distance):
            pl.semaphore_signal(
                barrier, inc=1, device_id={"seq": lax.rem(to, shards)}, device_id_type=MESH
            )
    for offset in range(1, owners):
        pl.semaphore_signal(
            barrier, inc=1, device_id={"head": lax.rem(owner + offset, owners)}, device_id_type=MESH
        )

    def slot_of(block):
        return {0: 0, prior: 1}.get(block, block + 1)

    def block_rows(block):
        return pl.ds(slot_of(block) * rows, rows)

    own = block_rows(prior)

    def own_copy(group, which):
        return pltpu.make_async_copy(
            (key_hbm, value_hbm)[which].at[:, pl.ds(group * HEAD_SIZE, HEAD_SIZE)],
            outer.at[group, own, pl.ds(which * HEAD_SIZE, HEAD_SIZE)],
            own_sem.at[group, which],
        )

    loads = [
        pltpu.make_async_copy(source, target, load_sem.at[i])
        for i, (source, target) in enumerate((
            (inner_key_hbm, inner_key_ref), (inner_value_hbm, inner_value_ref),
            (query_hbm, query_ref),
        ))
    ]
    for load in loads:
        load.start()
    for group in range(groups):
        for which in range(2):
            own_copy(group, which).start()
    weight_copy = pltpu.make_async_copy(weight_hbm, weight, weight_sem)
    weight_copy.start()
    for load in loads:
        load.wait()
    for group in range(groups):
        for which in range(2):
            own_copy(group, which).wait()

    pl.semaphore_wait(barrier, 2 * (1 + len(direct)) + owners - 1)

    def tail_copy(which):
        source, target = ((inner_key_ref, tail_keys), (inner_value_ref, tail_values))[which]
        return pltpu.make_async_remote_copy(
            src_ref=source.at[pl.ds(rows - span, span), :],
            dst_ref=target,
            send_sem=tail_send.at[which],
            recv_sem=tail_recv.at[which],
            device_id={"seq": lax.rem(shard + 1, shards)},
            device_id_type=MESH,
        )

    def outer_copy(group, distance):
        keys_values = pl.ds(0, 2 * HEAD_SIZE)
        return pltpu.make_async_remote_copy(
            src_ref=outer.at[group, own, keys_values],
            dst_ref=outer.at[group, block_rows(prior - distance), keys_values],
            send_sem=outer_send.at[group, distance - 1],
            recv_sem=outer_recv.at[group, distance - 1],
            device_id={"seq": lax.rem(shard + distance, shards)},
            device_id_type=MESH,
        )

    @pl.when(shard + 1 < shards)
    def _():
        tail_copy(0).start()
        tail_copy(1).start()

    even = lax.rem(shard, 2) == 0

    def hand_on(group, distance, to_distance, to):
        keys_values = pl.ds(0, 2 * HEAD_SIZE)
        return pltpu.make_async_remote_copy(
            src_ref=outer.at[group, block_rows(prior - distance), keys_values],
            dst_ref=outer.at[group, block_rows(prior - to_distance), keys_values],
            send_sem=hand_send.at[group, distance // 2],
            recv_sem=outer_recv.at[group, to_distance - 1],
            device_id={"seq": to},
            device_id_type=MESH,
        )

    def hand_up(group, distance):
        return hand_on(group, distance, distance + 1, lax.rem(shard + 1, shards))

    def hand_down(group, distance):
        return hand_on(group, distance, distance - 1, lax.rem(shard + shards - 1, shards))

    for group in range(groups):
        @pl.when(even)
        def _():
            hand_up(group, 0).start()

        for distance in reversed(direct):
            @pl.when(shard + distance < shards)
            def _():
                outer_copy(group, distance).start()

    def relay(group):
        for distance in direct:
            @pl.when(shard >= distance)
            def _():
                outer_copy(group, distance).wait_recv()
                if distance < prior:
                    @pl.when(even)
                    def _():
                        hand_up(group, distance).start()

                @pl.when(jnp.logical_not(even))
                def _():
                    hand_down(group, distance).start()

    for group in range(groups):
        columns = slice(group * HEAD_SIZE, (group + 1) * HEAD_SIZE)
        inner_keys[group, span:, :] = inner_key_ref[:, columns].astype(jnp.float32)
        inner_values[group, span:, :] = inner_value_ref[:, columns].astype(jnp.float32)

    @pl.when(shard == 0)
    def _():
        for group in range(groups):
            first = inner_keys[group, span : span + 1, :]
            inner_keys[group, :span, :] = jnp.broadcast_to(first, (span, HEAD_SIZE))
            inner_values[group, :span, :] = jnp.zeros((span, HEAD_SIZE), jnp.float32)

    @pl.when(shard > 0)
    def _():
        tail_copy(0).wait_recv()
        tail_copy(1).wait_recv()
        for group in range(groups):
            columns = slice(group * HEAD_SIZE, (group + 1) * HEAD_SIZE)
            inner_keys[group, :span, :] = tail_keys[:, columns].astype(jnp.float32)
            inner_values[group, :span, :] = tail_values[:, columns].astype(jnp.float32)

    count_rows = flipped.shape[1] - HEAD_SIZE

    def flip(group, block):
        there = slice(slot_of(block) * rows, (slot_of(block) + 1) * rows)
        value = outer[group, block_rows(block), HEAD_SIZE:].astype(jnp.float32)
        flipped[group, :HEAD_SIZE, there] = value.T.astype(jnp.bfloat16)
        flipped[group, HEAD_SIZE:, there] = jnp.ones((count_rows, rows), jnp.bfloat16)

    def receive(group):
        flip(group, prior)
        for distance in range(1, prior + 1):
            @pl.when(shard >= distance)
            def _():
                if distance % 2:
                    outer_copy(group, distance).wait_recv()
                flip(group, prior - distance)

        for place in range(prior):
            @pl.when(shard == place)
            def _():
                first = outer[group, block_rows(prior - place), :HEAD_SIZE][:1]
                for block in range(prior - place):
                    there = slice(slot_of(block) * rows, (slot_of(block) + 1) * rows)
                    outer[group, block_rows(block), :HEAD_SIZE] = jnp.broadcast_to(
                        first, (rows, HEAD_SIZE)
                    )
                    flipped[group, :, there] = jnp.zeros((flipped.shape[1], rows), jnp.bfloat16)

    lanes = LAGS_PER_STEP * CHUNK_ROWS
    pair_index = lax.broadcasted_iota(jnp.int32, (rows, lanes), 1)
    ahead = lax.broadcasted_iota(jnp.int32, (rows, lanes), 0) - lax.rem(pair_index, CHUNK_ROWS)
    pair_index = lax.broadcasted_iota(jnp.int32, (8, lanes), 1)
    behind = lax.rem(pair_index, CHUNK_ROWS) - lax.div(pair_index, CHUNK_ROWS)
    contract_last = (((1,), (1,)), ((), ()))

    def place_of(item):
        group = lax.rem(item, groups)
        first_row = pl.multiple_of(lax.div(item, groups) * CHUNK_ROWS, CHUNK_ROWS)
        return group, first_row

    def windows_of(array, group, first_row, step):
        start = span + first_row - step * LAGS_PER_STEP
        return [array[group, pl.ds(start - i, CHUNK_ROWS), :] for i in range(LAGS_PER_STEP)]

    def head_columns(group, head):
        return pl.ds(pl.multiple_of((group * heads + head) * HEAD_SIZE, HEAD_SIZE), HEAD_SIZE)

    def by_eight(array):
        return array.reshape(array.shape[0] // 8, 8, array.shape[1])

    def score_step(item, step, tops):
        group, first_row = place_of(item)
        oldest = ahead > first_row
        windows = windows_of(inner_keys, group, first_row, step)
        keys = outer[group, :, :HEAD_SIZE]
        result = []
        for head in range(heads):
            query = query_ref[pl.ds(first_row, CHUNK_ROWS), head_columns(group, head)]
            query = query.astype(jnp.float32)
            blended = jnp.concatenate(
                [(query * window).astype(jnp.bfloat16) for window in windows], axis=0
            )
            product = lax.dot_general(
                keys, blended, contract_last, preferred_element_type=jnp.float32
            )
            both = jnp.where(oldest, product[:rows], product[rows : 2 * rows])
            rest = product[2 * rows :]
            scores[head, step, :rows, :] = both
            scores[head, step, rows:, :] = rest
            top = jnp.maximum(jnp.max(by_eight(both), axis=0), jnp.max(by_eight(rest), axis=0))
            result.append(jnp.maximum(tops[head], top))
        return tuple(result)

    def value_step(item, step, tops, totals):
        group, first_row = place_of(item)
        oldest = ahead > first_row
        windows = jnp.concatenate(windows_of(inner_values, group, first_row, step), axis=0).T
        counted = (behind + first_row >= step * LAGS_PER_STEP) | (shard > 0)
        counted = jnp.where(counted, 1.0, 0.0)
        result = []
        for head in range(heads):
            total, count = totals[head]
            part = by_eight(scores[head, step])
            part = jnp.exp2((part - tops[head][None]) * factor).reshape(prior * rows, lanes)
            edge = part[:rows]
            weights = jnp.concatenate(
                [
                    jnp.where(oldest, edge, 0.0).astype(jnp.bfloat16),
                    jnp.where(oldest, 0.0, edge).astype(jnp.bfloat16),
                    part[rows:].astype(jnp.bfloat16),
                ],
                axis=0,
            )
            summed = jnp.dot(flipped[group], weights, preferred_element_type=jnp.float32)
            gain = windows * summed[:HEAD_SIZE]
            pairs = counted * summed[HEAD_SIZE : HEAD_SIZE + 8]
            for start in range(0, lanes, HEAD_SIZE):
                total = total + gain[:, start : start + HEAD_SIZE]
                count = count + pairs[:, start : start + HEAD_SIZE]
            result.append((total, count))
        return tuple(result)

    lowest = (jnp.full((8, lanes), -jnp.inf, jnp.float32),) * heads
    nothing = (
        (
            jnp.zeros((HEAD_SIZE, HEAD_SIZE), jnp.float32),
            jnp.zeros((8, HEAD_SIZE), jnp.float32),
        ),
    ) * heads

    def fold(array, combine):
        shift = CHUNK_ROWS
        while shift < HEAD_SIZE:
            array = combine(array, pltpu.roll(array, shift, 1))
            shift *= 2
        return array

    def finish_tops(tops):
        result = []
        for top in tops:
            most = top[:, :HEAD_SIZE]
            for start in range(HEAD_SIZE, lanes, HEAD_SIZE):
                most = jnp.maximum(most, top[:, start : start + HEAD_SIZE])
            most = jnp.max(fold(most, jnp.maximum), axis=0, keepdims=True)
            most = jnp.broadcast_to(most, (8, HEAD_SIZE))
            result.append(jnp.concatenate([most] * (lanes // HEAD_SIZE), axis=1))
        return tuple(result)

    def part_copy(offset, first_row):
        chunk = lax.div(first_row, CHUNK_ROWS)
        at = pl.ds(first_row, CHUNK_ROWS)
        return pltpu.make_async_remote_copy(
            src_ref=partial.at[offset, at, :],
            dst_ref=landed.at[offset - 1, at, :],
            send_sem=part_send.at[offset - 1, chunk],
            recv_sem=part_recv.at[offset - 1, chunk],
            device_id={"head": lax.rem(owner + offset, owners)},
            device_id_type=MESH,
        )

    def finish_item(item, totals):
        group, first_row = place_of(item)
        for head in range(heads):
            total, count = (fold(array, jnp.add) for array in totals[head])
            mean = (by_eight(total) / count[None]).reshape(total.shape).T
            attended[:, head_columns(group, head)] = mean[:CHUNK_ROWS].astype(jnp.bfloat16)

        @pl.when(group == groups - 1)
        def _():
            @pl.when(first_row == 0)
            def _():
                weight_copy.wait()

            for offset in list(range(1, owners)) + [0]:
                to = lax.rem(owner + offset, owners)
                columns = pl.ds(pl.multiple_of(to * own_width, own_width), own_width)
                partial[offset, pl.ds(first_row, CHUNK_ROWS), :] = jnp.dot(
                    attended[...], weight[:, columns], preferred_element_type=jnp.float32
                ).astype(jnp.bfloat16)
                if offset:
                    part_copy(offset, first_row).start()

    relay(0)
    receive(0)
    half = steps // 2
    for start in (0, half):
        if start:
            relay(1)
        else:
            tops = lowest
        tops = lax.fori_loop(
            start, start + half, lambda step, tops: score_step(0, step, tops), tops
        )
    def both_passes(item, tops):
        for group in range(1, groups):
            @pl.when(item == group)
            def _():
                receive(group)

        before = finish_tops(tops)

        def step_of(step, carry):
            now, totals = carry
            totals = value_step(item - 1, step, before, totals)
            return score_step(item, step, now), totals

        def half_of(which, carry):
            for group in range(2, groups):
                @pl.when((item == group - 1) & (which == 1))
                def _():
                    relay(group)

            return lax.fori_loop(which * half, (which + 1) * half, step_of, carry)

        tops, totals = lax.fori_loop(0, 2, half_of, (lowest, nothing))
        finish_item(item - 1, totals)
        return tops

    items = groups * chunks
    tops = lax.fori_loop(1, items, both_passes, tops)
    before = finish_tops(tops)
    totals = lax.fori_loop(
        0, steps, lambda step, totals: value_step(items - 1, step, before, totals), nothing
    )
    finish_item(items - 1, totals)

    for group in range(groups):
        @pl.when(even)
        def _():
            hand_up(group, 0).wait_send()

        for distance in direct:
            @pl.when(shard + distance < shards)
            def _():
                outer_copy(group, distance).wait_send()

            @pl.when(shard >= distance)
            def _():
                if distance < prior:
                    @pl.when(even)
                    def _():
                        hand_up(group, distance).wait_send()

                @pl.when(jnp.logical_not(even))
                def _():
                    hand_down(group, distance).wait_send()

    @pl.when(shard + 1 < shards)
    def _():
        tail_copy(0).wait_send()
        tail_copy(1).wait_send()

    for chunk in range(chunks):
        first_row = chunk * CHUNK_ROWS
        at = pl.ds(first_row, CHUNK_ROWS)
        total = partial[0, at, :].astype(jnp.float32)
        for offset in range(1, owners):
            part_copy(offset, first_row).wait_recv()
            total = total + landed[offset - 1, at, :].astype(jnp.float32)
        out_ref[at, :] = total.astype(out_ref.dtype)
    for chunk in range(chunks):
        for offset in range(1, owners):
            part_copy(offset, chunk * CHUNK_ROWS).wait_send()


def local(shards, owners, queries, first_keys, first_values, inner_keys, inner_values, out_weight):
    rows = queries.shape[0]
    groups = first_keys.shape[1] // HEAD_SIZE
    heads = queries.shape[1] // first_keys.shape[1]
    prior = W1 // rows
    outer = W1 + rows
    inner = W2 + rows
    features = out_weight.shape[1]
    chunks = rows // CHUNK_ROWS
    pairs = heads * groups * W2 * rows
    vmem = pl.BlockSpec(memory_space=pltpu.VMEM)
    dma = pltpu.SemaphoreType.DMA
    return pl.pallas_call(
        functools.partial(layer_kernel, shards, owners),
        out_shape=jax.ShapeDtypeStruct((rows, features // owners), queries.dtype),
        in_specs=[pl.BlockSpec(memory_space=pltpu.HBM)] * 6,
        out_specs=vmem,
        scratch_shapes=[
            pltpu.VMEM(queries.shape, jnp.bfloat16),
            pltpu.VMEM(inner_keys.shape, jnp.bfloat16),
            pltpu.VMEM(inner_keys.shape, jnp.bfloat16),
            pltpu.VMEM((groups, outer, 2 * HEAD_SIZE), jnp.bfloat16),
            pltpu.VMEM((groups, HEAD_SIZE + 16, outer), jnp.bfloat16),
            pltpu.VMEM((W2, groups * HEAD_SIZE), jnp.bfloat16),
            pltpu.VMEM((W2, groups * HEAD_SIZE), jnp.bfloat16),
            pltpu.VMEM((groups, inner, HEAD_SIZE), jnp.float32),
            pltpu.VMEM((groups, inner, HEAD_SIZE), jnp.float32),
            pltpu.VMEM(
                (heads, W2 // LAGS_PER_STEP, W1, LAGS_PER_STEP * CHUNK_ROWS), jnp.float32
            ),
            pltpu.VMEM((CHUNK_ROWS, queries.shape[1]), jnp.bfloat16),
            pltpu.VMEM(out_weight.shape, jnp.bfloat16),
            pltpu.VMEM((owners, rows, features // owners), jnp.bfloat16),
            pltpu.VMEM((owners - 1, rows, features // owners), jnp.bfloat16),
            dma((groups, prior)),
            dma((groups, prior)),
            dma((2,)),
            dma((2,)),
            dma((owners - 1, chunks)),
            dma((owners - 1, chunks)),
            dma(()),
            dma((3,)),
            dma((groups, 2)),
            dma((groups, prior // 2 + 1)),
        ],
        compiler_params=pltpu.CompilerParams(
            collective_id=0, has_side_effects=True, vmem_limit_bytes=64 * 1024 * 1024 - 2**17
        ),
        cost_estimate=pl.CostEstimate(
            flops=4 * pairs * outer * HEAD_SIZE + 2 * rows * out_weight.size,
            bytes_accessed=2 * out_weight.size,
            transcendentals=pairs * W1,
        ),
    )(queries, first_keys, first_values, inner_keys, inner_values, out_weight)


def solution(mesh):
    in_specs = (P("seq", "head"),) * 5 + (P("head", None),)
    return jax.shard_map(
        functools.partial(local, mesh.shape["seq"], mesh.shape["head"]),
        mesh=mesh, in_specs=in_specs, out_specs=P("seq", "head"), check_vma=False,
    )
```
